256 devices in a mesh: dp: 256 (over x, z, y, core).
Axes of the slice: x: 4, y: 4, z: 8, core: 2. Of those that a mesh axis runs over, the one named last changes fastest.
Arguments:
- image_features: bfloat16 [32768, 1152], P('dp'), may hold values from -0.59765625 to 0.59765625
- text_features: bfloat16 [32768, 1152], P('dp'), may hold values from -0.59765625 to 0.59765625
- projections: bfloat16 [2304, 1152], P('dp'), may hold values from -0.1875 to 0.1875
- labels: int32 [32768], P('dp'), may hold values from 0 to 32767, as said below
Outputs:
- image_grad: float32 [32768, 1152], P('dp')
- text_grad: float32 [32768, 1152], P('dp')
The draws below stay inside these ranges and needn't reach their ends.
Inputs may be any that keep to these rules, and one draw needn't show every extreme that they name: For each block k of 128 rows, the labels are the 128 text rows of one block (k - s) mod 256, each once, with s between 0 and 31 drawn for each block.
All inputs are finite; a program needn't handle non-finite values.
Results may differ from the reference program's by a relative error of at most 0.01.
Values may be sent and summed in bfloat16 or wider, within the bound.
No kernel may reach another device: no remote copies, remote signals or barrier semaphores. Data moves between devices by JAX's collectives and lax.ppermute only.
A program may use at most 128 MiB of HBM per device.

```python
import jax
import jax.numpy as jnp
from jax import lax

DIN = 1152
D = 1152
ROWS = 128
BLOCKS = 256
SHIFTS = 32
BATCH = 32768


def draw_labels(key, part):
    first, second = jax.random.split(jax.random.fold_in(key, 17))
    offsets = jax.random.randint(first, (BLOCKS,), 0, SHIFTS)
    keys = jax.random.split(second, BLOCKS)
    orders = jax.vmap(lambda one: jax.random.permutation(one, ROWS))(keys)
    sources = (jnp.arange(BLOCKS, dtype=jnp.int32) - offsets) % BLOCKS
    return (sources[:, None] * ROWS + orders).reshape(-1).astype(jnp.int32)


def level_of(own_key, extent, cuts, low, largest):
    gain = 1.0
    for axis_at, blocks in cuts:
        steps = jax.random.uniform(jax.random.fold_in(jax.random.fold_in(own_key, 6), axis_at), (blocks,), jnp.float32, low / len(cuts), largest / len(cuts))
        gain = gain * jnp.repeat(jnp.exp(steps), extent[axis_at] // blocks).reshape((-1,) + (1,) * (len(extent) - 1 - axis_at))
    return gain


def noise(rng, extent, deviation, reach, cuts=(), kind=jnp.bfloat16):
    result = jax.random.normal(rng, extent, jnp.float32) * deviation
    if len(cuts) > 0:
        result = level_of(rng, extent, cuts, -0.22, 0.18) * result
    return jnp.clip(result, min=-reach, max=reach).astype(kind)


def setup_inputs(seed: int = 0) -> dict:
    key_of = jax.random.split(jax.random.key(seed), 5)
    image_features = noise(key_of[0], (BATCH, DIN), 0.1, 0.59765625, ((0, 256),))
    text_features = noise(key_of[1], (BATCH, DIN), 0.1, 0.59765625, ((0, 256),))
    projections = noise(key_of[2], (2 * DIN, D), DIN ** -0.5, 0.1875, ((0, 256),))
    labels = draw_labels(jax.random.fold_in(key_of[4], 71), 0)
    return {"image_features": image_features, "text_features": text_features, "projections": projections, "labels": labels}


logit_scale = 10.0
logit_bias = -2.0
eps = 1e-06

def normalize(raw):
    norm = jnp.sqrt(lax.optimization_barrier(jnp.sum(raw * raw, axis=-1, keepdims=True)) + eps)
    return (raw / norm, norm)

def unproject(unit, norm, grad):
    inner = lax.optimization_barrier(jnp.sum(unit * grad, axis=-1, keepdims=True))
    return ((grad - unit * inner) / norm).astype(jnp.bfloat16)

def reference(image_features, text_features, projections, labels):
    width_in = image_features.shape[1]
    image_weight = projections[:width_in]
    text_weight = projections[width_in:]
    image_unit, image_norm = normalize(jnp.dot(image_features, image_weight, preferred_element_type=jnp.float32))
    text_unit, text_norm = normalize(jnp.dot(text_features, text_weight, preferred_element_type=jnp.float32))
    image_emb = image_unit.astype(jnp.bfloat16)
    text_emb = text_unit.astype(jnp.bfloat16)
    width = image_emb.shape[1]
    image_blocks = image_emb.astype(jnp.float32).reshape(BLOCKS, ROWS, width)
    text_all = text_emb.astype(jnp.float32)
    label_blocks = labels.reshape(BLOCKS, ROWS)
    positions = jnp.arange(ROWS, dtype=jnp.int32)
    owners = jnp.arange(BLOCKS, dtype=jnp.int32)

    def one_offset(offset, state):
        image_acc, text_acc = state
        offset = jnp.asarray(offset).astype(jnp.int32)
        paired = jnp.roll(text_all, offset * ROWS, axis=0).reshape(BLOCKS, ROWS, width)
        text_ids = ((owners - offset) % BLOCKS)[:, None] * ROWS + positions[None, :]
        logits = logit_scale * jnp.einsum('kid,kjd->kij', image_blocks, paired) + logit_bias
        positive = (label_blocks[:, :, None] == text_ids[:, None, :]).astype(jnp.float32)
        coeff_low = (jax.nn.sigmoid(logits) - positive).astype(jnp.bfloat16)
        coeff = lax.optimization_barrier(coeff_low).astype(jnp.float32)
        image_acc = image_acc + logit_scale * jnp.einsum('kij,kjd->kid', coeff, paired)
        text_part = logit_scale * jnp.einsum('kij,kid->kjd', coeff, image_blocks).reshape(BLOCKS * ROWS, width)
        text_acc = text_acc + jnp.roll(text_part, -offset * ROWS, axis=0)
        return (image_acc, text_acc)
    start = (jnp.zeros((BLOCKS, ROWS, width), jnp.float32), jnp.zeros((BLOCKS * ROWS, width), jnp.float32))
    image_acc, text_acc = lax.fori_loop(0, SHIFTS, one_offset, start)
    image_draw = unproject(image_unit, image_norm, image_acc.reshape(BLOCKS * ROWS, width))
    text_draw = unproject(text_unit, text_norm, text_acc)
    image_grad = jnp.dot(image_draw, image_weight.T, preferred_element_type=jnp.float32)
    text_grad = jnp.dot(text_draw, text_weight.T, preferred_element_type=jnp.float32)
    return (image_grad, text_grad)
```

```python
import jax
import jax.numpy as jnp
from jax import lax
from jax.sharding import Mesh, PartitionSpec as P

AXES = ("x", "z", "y", "c")
SIZES = (4, 8, 4, 2)
WINDOW_PLANES = 4

logit_scale = 10.0
logit_bias = -2.0
eps = 1e-06
contract_last = (((1,), (1,)), ((), ()))
contract_first = (((0,), (0,)), ((), ()))


def along(value, axis, steps):
    count = lax.axis_size(axis)
    return lax.ppermute(value, axis, [(i, (i + steps) % count) for i in range(count)])


def blocks_behind(value, steps):
    return lax.ppermute(value, AXES, [(i, (i + steps) % 256) for i in range(256)])


def normalize(raw):
    norm = jnp.sqrt(jnp.sum(raw * raw, axis=-1, keepdims=True) + eps)
    return (raw / norm, norm)


def unproject(unit, norm, grad):
    inner = jnp.sum(unit * grad, axis=-1, keepdims=True)
    return ((grad - unit * inner) / norm).astype(jnp.bfloat16)


def gather_images(value):
    same = [value, along(value, "y", -1), along(value, "y", 2), along(value, "y", 1)]
    other = [along(v, "c", 1) for v in same]
    return [v for pair in zip(same, other) for v in pair]


def gather_labels(labels):
    pair = jnp.stack([labels, along(labels, "c", 1)])
    around = [pair, along(pair, "y", -1), along(pair, "y", 2), along(pair, "y", 1)]
    return jnp.concatenate(around, axis=0)


def per_device(image_features, text_features, projections, labels):
    rows, width_in = image_features.shape
    x, z, y, c = (lax.axis_index(a) for a in AXES)
    index = lax.axis_index(AXES)
    place = 2 * y + c

    whole = lax.all_gather(projections, AXES, axis=0, tiled=True)
    image_weight = whole[:width_in]
    text_weight = whole[width_in:]

    texts = [text_features]
    for _ in range(WINDOW_PLANES):
        texts.append(blocks_behind(texts[-1], 8))
    images = gather_images(image_features)
    label_slots = gather_labels(labels)

    image_raw = jnp.dot(jnp.concatenate(images, axis=0), image_weight, preferred_element_type=jnp.float32)
    text_raw = jnp.dot(jnp.concatenate(texts, axis=0), text_weight, preferred_element_type=jnp.float32)
    image_unit, image_norm = normalize(image_raw)
    text_unit, text_norm = normalize(text_raw)
    image_emb = image_unit.astype(jnp.bfloat16)
    text_emb = text_unit.astype(jnp.bfloat16)

    slots = jnp.arange(8, dtype=jnp.int32)
    slot_place = 2 * ((y + slots // 2) % 4) + (c + slots) % 2
    planes = jnp.arange(WINDOW_PLANES + 1, dtype=jnp.int32)
    valid = jnp.where(
        planes[None, :] == 0,
        slot_place[:, None] >= place,
        (planes[None, :] < WINDOW_PLANES) | (slot_place[:, None] < place),
    )
    text_ids = ((index - 8 * planes) % 256)[:, None] * rows + jnp.arange(rows, dtype=jnp.int32)
    text_ids = text_ids.reshape(1, 1, WINDOW_PLANES + 1, rows)
    logits = (
        logit_scale
        * lax.dot_general(image_emb, text_emb, contract_last, preferred_element_type=jnp.float32)
        + logit_bias
    ).reshape(8, rows, WINDOW_PLANES + 1, rows)
    positive = (label_slots[:, :, None, None] == text_ids).astype(jnp.float32)
    coeff = jnp.where(valid[:, None, :, None], jax.nn.sigmoid(logits) - positive, 0.0)
    coeff = coeff.astype(jnp.bfloat16).reshape(8 * rows, (WINDOW_PLANES + 1) * rows)

    text_part = lax.dot_general(coeff, image_emb, contract_first, preferred_element_type=jnp.float32)
    image_part = jnp.dot(coeff, text_emb, preferred_element_type=jnp.float32)

    text_part = text_part.reshape(WINDOW_PLANES + 1, rows, -1)
    carried = text_part[WINDOW_PLANES]
    for plane in range(WINDOW_PLANES - 1, -1, -1):
        carried = blocks_behind(carried.astype(jnp.bfloat16), -8).astype(jnp.float32) + text_part[plane]
    text_acc = logit_scale * carried

    image_part = image_part.reshape(4, 2, rows, -1)
    swapped = along(image_part[:, 1].astype(jnp.bfloat16), "c", 1).astype(jnp.float32)
    chip_sum = image_part[:, 0] + swapped
    outgoing = chip_sum.astype(jnp.bfloat16)
    image_acc = chip_sum[0]
    for dy, steps in ((1, 1), (2, 2), (3, -1)):
        image_acc = image_acc + along(outgoing[dy], "y", steps).astype(jnp.float32)
    image_acc = logit_scale * image_acc

    image_draw = unproject(image_unit[:rows], image_norm[:rows], image_acc)
    text_draw = unproject(text_unit[:rows], text_norm[:rows], text_acc)
    image_grad = lax.dot_general(image_draw, image_weight, contract_last, preferred_element_type=jnp.float32)
    text_grad = lax.dot_general(text_draw, text_weight, contract_last, preferred_element_type=jnp.float32)
    return (image_grad, text_grad)


def solution(mesh):
    fine = Mesh(mesh.devices.reshape(SIZES), AXES)
    rows = P(AXES, None)
    return jax.shard_map(
        per_device,
        mesh=fine,
        in_specs=(rows, rows, rows, P(AXES)),
        out_specs=(rows, rows),
        check_vma=False,
    )
```

```python
import jax
import jax.numpy as jnp
from jax import lax
from jax.experimental import pallas as pl
from jax.experimental.pallas import tpu as pltpu
from jax.sharding import Mesh, PartitionSpec as P

AXES = ("x", "z", "y", "c")
SIZES = (4, 8, 4, 2)
WINDOW_PLANES = 4

logit_scale = 10.0
logit_bias = -2.0
eps = 1e-06
contract_last = (((1,), (1,)), ((), ()))
contract_first = (((0,), (0,)), ((), ()))


def along(value, axis, steps):
    count = lax.axis_size(axis)
    return lax.ppermute(value, axis, [(i, (i + steps) % count) for i in range(count)])


def blocks_behind(value, steps):
    return lax.ppermute(value, AXES, [(i, (i + steps) % 256) for i in range(256)])


def device(x, z, y, c):
    return ((x * 8 + z) * 4 + y) * 2 + c


def everyone():
    return [(x, z, y, c) for x in range(4) for z in range(8) for y in range(4) for c in range(2)]


def crosswise(value, core0_axis, steps):
    pairs = []
    for x, z, y, c in everyone():
        if (core0_axis == "x") == (c == 0):
            source = device((x + steps) % 4, z, y, c)
        else:
            source = device(x, z, (y + steps) % 4, c)
        pairs.append((source, device(x, z, y, c)))
    return lax.ppermute(value, AXES, pairs)


def order_shards(where_ref, *refs):
    chips, out_ref, wide_ref = refs[:4], refs[4], refs[5]
    height = chips[0].shape[0] // 2
    for n in range(8):
        slot = 2 * lax.rem(where_ref[0] + n // 2, 4) + lax.rem(where_ref[1] + n % 2, 2)
        shard = chips[n // 2][...].astype(jnp.float32)
        for row in range(height):
            at = n % 2 * height + row
            wide_ref[pl.ds(slot * height + row, 1), :] = shard[at : at + 1]
    out_ref[...] = wide_ref[...].astype(out_ref.dtype)


def order_units(where_ref, *refs):
    units, out_ref, wide_ref = refs[:4], refs[4], refs[5]
    height = units[0].shape[0]
    for n, unit_ref in enumerate(units):
        at = pl.multiple_of(lax.rem(where_ref[0] + n, 4) * height, 8)
        wide_ref[pl.ds(at, height), :] = unit_ref[...].astype(jnp.float32)
    out_ref[...] = wide_ref[...].astype(out_ref.dtype)


def on_device(body, where, arrays, outs, scratch=(), flops=0):
    out_bytes = sum(o.size * o.dtype.itemsize for o in outs) + sum(v.size * v.dtype.itemsize for v in arrays)
    return pl.pallas_call(
        body,
        out_shape=outs,
        in_specs=[pl.BlockSpec(memory_space=pltpu.SMEM)] + [pl.BlockSpec(memory_space=pltpu.VMEM)] * len(arrays),
        out_specs=[pl.BlockSpec(memory_space=pltpu.VMEM)] * len(outs),
        scratch_shapes=list(scratch),
        compiler_params=pltpu.CompilerParams(vmem_limit_bytes=50 << 20),
        cost_estimate=pl.CostEstimate(flops=flops, bytes_accessed=out_bytes, transcendentals=0),
    )(jnp.stack(where).astype(jnp.int32), *arrays)


def like(rows, width, dtype):
    return jax.ShapeDtypeStruct((rows, width), dtype)


def unit_place(x, z, y, c):
    high, low = (x % 2) * 2 + z // 4, z % 4
    tx, ty = ((high + 3) % 4, low) if x < 2 else (low, high)
    far = [z, z + 1, z - 1, z + 2, z - 2, z + 3, z - 3, z + 4]
    rank = 2 * {0: 3, 1: 1, 3: 2, 2: 0}[(y - ty) % 4] + c
    return (tx, far[rank] % 8, ty, x // 2)


def start_weights(shard):
    y, c = lax.axis_index("y"), lax.axis_index("c")
    chip = jnp.concatenate([shard, along(shard, "c", 1)])
    chips = [chip, along(chip, "y", -1), along(chip, "y", 2), along(chip, "y", 1)]
    height, width = 4 * chip.shape[0], chip.shape[1]
    (unit,) = on_device(
        order_shards, (y, c), chips, [like(height, width, shard.dtype)], [pltpu.VMEM((height, width), jnp.float32)]
    )
    return unit


def spread_units(unit):
    pairs = [(device(*source), device(*unit_place(*source))) for source in everyone()]
    return lax.ppermute(unit, AXES, pairs)


def gather_block(unit):
    x, y, c = lax.axis_index("x"), lax.axis_index("y"), lax.axis_index("c")
    near = [unit] + [crosswise(unit, "y", d) for d in (1, 2, 3)]
    height, width = 4 * unit.shape[0], unit.shape[1]
    (block,) = on_device(
        order_units, (jnp.where(c == 0, y, x),), near, [like(height, width, unit.dtype)],
        [pltpu.VMEM((height, width), jnp.float32)],
    )
    return block


def project(where_ref, *refs):
    pieces, images, texts = refs[:8], refs[8:16], refs[16:21]
    (image_weight, text_weight, image_emb, text_emb, coeff_ref, far_ref,
     image_unit, image_norm, text_unit, text_norm) = refs[21:]
    core, own_first, other_first, y = where_ref[0], where_ref[1], where_ref[2], where_ref[3]
    block = pieces[0].shape[0]
    rows, width = texts[0].shape

    def put(own_ref, other_ref):
        for n in range(8):
            target, first = (own_ref, own_first) if n < 4 else (other_ref, other_first)
            at = pl.multiple_of(lax.rem(first + n % 4, 4) * block, 32)
            target[pl.ds(at, block), :] = pieces[n][...]

    @pl.when(core == 0)
    def _():
        put(image_weight, text_weight)

    @pl.when(core != 0)
    def _():
        put(text_weight, image_weight)

    def embed(sources, weight, emb, first, unit_ref, norm_ref):
        features = jnp.concatenate([source[:, :width] for source in sources])
        unit, norm = normalize(jnp.dot(features, weight[...], preferred_element_type=jnp.float32))
        emb[pl.ds(first * rows, len(sources) * rows), :] = unit.astype(jnp.bfloat16)
        if first == 0:
            unit_ref[...] = unit[:rows]
            norm_ref[...] = jnp.broadcast_to(norm[:rows], norm_ref.shape)

    for first in (0, 2, 4, 6):
        embed(images[first : first + 2], image_weight, image_emb, first, image_unit, image_norm)
    for first in (0, 2, 4):
        embed(texts[first : first + 2], text_weight, text_emb, first, text_unit, text_norm)

    column = lax.broadcasted_iota(jnp.int32, (rows, rows), 1)
    place = 2 * y + core
    for first in (0, 2, 4, 6):
        logits = logit_bias + logit_scale * lax.dot_general(
            image_emb[pl.ds(first * rows, 2 * rows), :], text_emb[...], contract_last,
            preferred_element_type=jnp.float32,
        )
        chance = jax.nn.sigmoid(logits)
        for slot in (first, first + 1):
            ahead = 2 * lax.rem(y + slot // 2, 4) + lax.rem(core + slot % 2, 2)
            marks = images[slot][:, width:].astype(jnp.float32).astype(jnp.int32)
            behind, label = marks[:, 0:1], marks[:, 1:2]
            hit = column == label
            for plane in range(WINDOW_PLANES + 1):
                distance = ahead + 8 * plane - place
                tile = chance[(slot - first) * rows : (slot - first + 1) * rows, plane * rows : (plane + 1) * rows]
                tile = tile - jnp.where(hit & (behind == distance), 1.0, 0.0)
                if plane in (0, WINDOW_PLANES):
                    tile = tile * jnp.where((distance >= 0) & (distance < 8 * WINDOW_PLANES), 1.0, 0.0)
                coeff_ref[slot * rows : (slot + 1) * rows, plane * rows : (plane + 1) * rows] = tile.astype(jnp.bfloat16)

    far_ref[...] = lax.dot_general(
        coeff_ref[:, WINDOW_PLANES * rows :], image_emb[...], contract_first, preferred_element_type=jnp.float32
    ).astype(far_ref.dtype)


def sum_pairs(where_ref, coeff_ref, image_emb, text_emb, *outs):
    rows = image_emb.shape[0] // 8
    text_sums, kept, sent_ref = outs[:4], outs[4:8], outs[8]
    for plane in range(WINDOW_PLANES):
        text_sums[plane][...] = lax.dot_general(
            coeff_ref[:, plane * rows : (plane + 1) * rows], image_emb[...], contract_first,
            preferred_element_type=jnp.float32,
        )
    for dy in range(4):
        both = jnp.dot(
            coeff_ref[2 * dy * rows : 2 * (dy + 1) * rows, :], text_emb[...], preferred_element_type=jnp.float32
        )
        kept[dy][...] = both[:rows]
        sent_ref[dy] = both[rows:].astype(sent_ref.dtype)


def finish(where_ref, sum_ref, unit_ref, norm_ref, weight_ref, *refs):
    arrived, grad_ref = refs[:-1], refs[-1]
    total = sum_ref[...]
    for one in arrived:
        total = total + one[...].astype(jnp.float32)
    draw = unproject(unit_ref[...], norm_ref[:, 0:1], logit_scale * total)
    grad_ref[...] = lax.dot_general(draw, weight_ref[...], contract_last, preferred_element_type=jnp.float32)


def normalize(raw):
    norm = jnp.sqrt(jnp.sum(raw * raw, axis=-1, keepdims=True) + eps)
    return (raw / norm, norm)


def unproject(unit, norm, grad):
    inner = jnp.sum(unit * grad, axis=-1, keepdims=True)
    return ((grad - unit * inner) / norm).astype(jnp.bfloat16)


def per_device(image_features, text_features, projections, labels):
    rows, width = image_features.shape
    x, z, y, c = (lax.axis_index(a) for a in AXES)
    index = lax.axis_index(AXES)
    tied = lax.optimization_barrier

    marks = jnp.stack([(index - labels // rows) % 256, labels % rows], axis=1).astype(image_features.dtype)
    marked = jnp.concatenate([image_features, jnp.pad(marks, ((0, 0), (0, 126)))], axis=1)

    texts = [text_features, blocks_behind(text_features, 8)]
    unit = start_weights(projections)
    unit, marked, hop = tied((unit, marked, texts[-1]))
    texts[-1] = hop
    unit = spread_units(unit)
    texts.append(blocks_behind(hop, 8))
    images = [marked, along(marked, "y", -1), along(marked, "y", 2), along(marked, "y", 1)]
    unit, hop = tied((unit, texts[-1]))
    texts[-1] = hop
    block = gather_block(unit)
    texts.append(blocks_behind(hop, 8))
    block, hop = tied((block, texts[-1]))
    texts[-1] = hop
    pieces = [block] + [crosswise(block, "x", d) for d in (1, 2, 3)]
    texts.append(blocks_behind(hop, 8))
    images = [v for mine in images for v in (mine, along(mine, "c", 1))]
    pieces = pieces + [along(piece, "c", 1) for piece in pieces]

    whole = like(4 * block.shape[0], width, block.dtype)
    first_x, first_y = (x + 1) % 4, y
    where = (c, jnp.where(c == 0, first_x, first_y), jnp.where(c == 0, first_y, first_x), y)
    wide, narrow = like(rows, width, jnp.float32), like(rows, 128, jnp.float32)
    low = jnp.bfloat16
    (image_weight, text_weight, image_emb, text_emb, coeff, far, image_unit, image_norm, text_unit, text_norm) = on_device(
        project, where, pieces + images + texts,
        [whole, whole, like(8 * rows, width, low), like(5 * rows, width, low), like(8 * rows, 5 * rows, low),
         like(rows, width, low), wide, narrow, wide, narrow],
        flops=2 * 13 * rows * width * width + 2 * 46 * rows * rows * width,
    )
    far = blocks_behind(far, -8)
    *sums, sent = on_device(
        sum_pairs, (y,), [coeff, image_emb, text_emb],
        [wide] * 8 + [jax.ShapeDtypeStruct((4, rows, width), low)],
        flops=2 * 72 * rows * rows * width,
    )
    text_sums, kept = sums[:4], sums[4:]

    swapped = along(sent, "c", 1)
    carried = (far.astype(jnp.float32) + text_sums[3]).astype(low)
    carried, swapped = tied((carried, swapped))
    far = blocks_behind(carried, -8)
    chip = [kept[dy] + swapped[dy].astype(jnp.float32) for dy in range(4)]
    arrived = [along(chip[dy].astype(low), "y", steps) for dy, steps in ((1, 1), (2, 2), (3, -1))]
    carried = (far.astype(jnp.float32) + text_sums[2]).astype(low)
    far = blocks_behind(carried, -8)
    carried = (far.astype(jnp.float32) + text_sums[1]).astype(low)
    far = blocks_behind(carried, -8)
    flops = 2 * rows * width * width
    (image_grad,) = on_device(finish, (y,), [chip[0], image_unit, image_norm, image_weight, *arrived], [wide], flops=flops)
    (text_grad,) = on_device(finish, (y,), [text_sums[0], text_unit, text_norm, text_weight, far], [wide], flops=flops)
    return (image_grad, text_grad)


def solution(mesh):
    fine = Mesh(mesh.devices.reshape(SIZES), AXES)
    rows = P(AXES, None)
    return jax.shard_map(
        per_device,
        mesh=fine,
        in_specs=(rows, rows, rows, P(AXES)),
        out_specs=(rows, rows),
        check_vma=False,
    )
```

```python
import jax
import jax.numpy as jnp
from jax import lax
from jax.experimental import pallas as pl
from jax.experimental.pallas import tpu as pltpu
from jax.sharding import Mesh, PartitionSpec as P

AXES = ("x", "z", "y", "c")
SIZES = (4, 8, 4, 2)
WINDOW_PLANES = 4

logit_scale = 10.0
logit_bias = -2.0
eps = 1e-06
contract_last = (((1,), (1,)), ((), ()))
contract_first = (((0,), (0,)), ((), ()))


def along(value, axis, steps):
    count = lax.axis_size(axis)
    return lax.ppermute(value, axis, [(i, (i + steps) % count) for i in range(count)])


def blocks_behind(value, steps):
    return lax.ppermute(value, AXES, [(i, (i + steps) % 256) for i in range(256)])


def device(x, z, y, c):
    return ((x * 8 + z) * 4 + y) * 2 + c


def everyone():
    return [(x, z, y, c) for x in range(4) for z in range(8) for y in range(4) for c in range(2)]


def crosswise(value, core0_axis, steps):
    pairs = []
    for x, z, y, c in everyone():
        if (core0_axis == "x") == (c == 0):
            source = device((x + steps) % 4, z, y, c)
        else:
            source = device(x, z, (y + steps) % 4, c)
        pairs.append((source, device(x, z, y, c)))
    return lax.ppermute(value, AXES, pairs)


def order_shards(where_ref, *refs):
    chips, out_ref, wide_ref = refs[:4], refs[4], refs[5]
    height = chips[0].shape[0] // 2
    for n in range(8):
        slot = 2 * lax.rem(where_ref[0] + n // 2, 4) + lax.rem(where_ref[1] + n % 2, 2)
        shard = chips[n // 2][...].astype(jnp.float32)
        for row in range(height):
            at = n % 2 * height + row
            wide_ref[pl.ds(slot * height + row, 1), :] = shard[at : at + 1]
    out_ref[...] = wide_ref[...].astype(out_ref.dtype)


def order_units(where_ref, *refs):
    units, out_ref, wide_ref = refs[:4], refs[4], refs[5]
    height = units[0].shape[0]
    for n, unit_ref in enumerate(units):
        at = pl.multiple_of(lax.rem(where_ref[0] + n, 4) * height, 8)
        wide_ref[pl.ds(at, height), :] = unit_ref[...].astype(jnp.float32)
    out_ref[...] = wide_ref[...].astype(out_ref.dtype)


def on_device(body, where, arrays, outs, scratch=(), flops=0, vmem=8, anywhere=0):
    out_bytes = sum(o.size * o.dtype.itemsize for o in outs) + sum(v.size * v.dtype.itemsize for v in arrays)
    return pl.pallas_call(
        body,
        out_shape=outs,
        in_specs=[pl.BlockSpec(memory_space=pltpu.SMEM)]
        + [pl.BlockSpec(memory_space=pl.ANY)] * anywhere
        + [pl.BlockSpec(memory_space=pltpu.VMEM)] * (len(arrays) - anywhere),
        out_specs=[pl.BlockSpec(memory_space=pltpu.VMEM)] * len(outs),
        scratch_shapes=list(scratch),
        compiler_params=pltpu.CompilerParams(vmem_limit_bytes=vmem << 20),
        cost_estimate=pl.CostEstimate(flops=flops, bytes_accessed=out_bytes, transcendentals=0),
    )(jnp.stack(where).astype(jnp.int32), *arrays)


def like(rows, width, dtype):
    return jax.ShapeDtypeStruct((rows, width), dtype)


def unit_place(x, z, y, c):
    high, low = (x % 2) * 2 + z // 4, z % 4
    tx, ty = ((high + 3) % 4, low) if x < 2 else (low, high)
    far = [z, z + 1, z - 1, z + 2, z - 2, z + 3, z - 3, z + 4]
    rank = 2 * {0: 3, 1: 1, 3: 2, 2: 0}[(y - ty) % 4] + c
    return (tx, far[rank] % 8, ty, x // 2)


def start_weights(shard):
    y, c = lax.axis_index("y"), lax.axis_index("c")
    chip = jnp.concatenate([shard, along(shard, "c", 1)])
    chips = [chip, along(chip, "y", -1), along(chip, "y", 2), along(chip, "y", 1)]
    height, width = 4 * chip.shape[0], chip.shape[1]
    (unit,) = on_device(
        order_shards, (y, c), chips, [like(height, width, shard.dtype)], [pltpu.VMEM((height, width), jnp.float32)]
    )
    return unit


def spread_units(unit):
    pairs = [(device(*source), device(*unit_place(*source))) for source in everyone()]
    return lax.ppermute(unit, AXES, pairs)


def gather_near(unit):
    return [unit] + [crosswise(unit, "y", d) for d in (1, 2, 3)]


def join_units(near):
    x, y, c = lax.axis_index("x"), lax.axis_index("y"), lax.axis_index("c")
    height, width = 4 * near[0].shape[0], near[0].shape[1]
    (block,) = on_device(
        order_units, (jnp.where(c == 0, y, x),), near, [like(height, width, near[0].dtype)],
        [pltpu.VMEM((height, width), jnp.float32)],
    )
    return block


def place(where_ref, on_core0, pieces, weight, sems):
    for core_is_0 in (True, False):

        @pl.when((where_ref[0] == 0) if core_is_0 else (where_ref[0] != 0))
        def _():
            own = core_is_0 == on_core0
            block = pieces[0].shape[0]
            first = where_ref[1] if own else where_ref[2]
            copies = []
            for n in range(4):
                at = pl.multiple_of(lax.rem(first + n, 4) * block, 32)
                piece = pieces[n if own else 4 + n]
                copies.append(pltpu.make_async_copy(piece, weight.at[pl.ds(at, block)], sems.at[n]))
            for copy in copies:
                copy.start()
            for copy in copies:
                copy.wait()


def embed(sources, weight, emb, unit_ref, norm_ref):
    rows, width = unit_ref.shape
    for first in range(0, len(sources), 2):
        some = sources[first : first + 2]
        features = jnp.concatenate([source[:, :width] for source in some])
        unit, norm = normalize(jnp.dot(features, weight[...], preferred_element_type=jnp.float32))
        emb[pl.ds(first * rows, len(some) * rows), :width] = unit.astype(jnp.bfloat16)
        if first == 0:
            unit_ref[...] = unit[:rows]
            norm_ref[...] = jnp.broadcast_to(norm[:rows], norm_ref.shape)


def embed_images(where_ref, *refs):
    weight, emb, unit_ref, norm_ref, sems = refs[12:]
    place(where_ref, True, refs[:8], weight, sems)
    images = refs[8:12]
    embed(images, weight, emb, unit_ref, norm_ref)
    rows, width = unit_ref.shape
    for slot, image in enumerate(images):
        emb[slot * rows : (slot + 1) * rows, width:] = image[:, width:]


def embed_texts(where_ref, *refs):
    weight, emb, unit_ref, norm_ref, sems = refs[13:]
    place(where_ref, False, refs[:8], weight, sems)
    embed(refs[8:13], weight, emb, unit_ref, norm_ref)


def text_sum(own_coeff, other_coeff, own_emb, other_emb, plane):
    width = own_emb.shape[1] - 128
    rows = own_emb.shape[0] // 4
    total = 0.0
    for coeff, emb in ((own_coeff, own_emb), (other_coeff, other_emb)):
        total = total + lax.dot_general(
            coeff[:, plane * rows : (plane + 1) * rows], emb[:, :width], contract_first,
            preferred_element_type=jnp.float32,
        )
    return total


def weigh_pairs(where_ref, own_emb, other_emb, text_emb, own_coeff, other_coeff, far_ref):
    core, y = where_ref[0], where_ref[3]
    rows, width = text_emb.shape[0] // 5, text_emb.shape[1]
    column = lax.broadcasted_iota(jnp.int32, (rows, rows), 1)
    for kind, (emb, coeff_ref) in enumerate(((own_emb, own_coeff), (other_emb, other_coeff))):
        for first in (0, 2):
            logits = logit_bias + logit_scale * lax.dot_general(
                emb[first * rows : (first + 2) * rows, :width], text_emb[...], contract_last,
                preferred_element_type=jnp.float32,
            )
            chance = jax.nn.sigmoid(logits)
            for slot in (first, first + 1):
                ahead = 2 * lax.rem(y + slot, 4) + lax.rem(core + kind, 2)
                at = slice(slot * rows, (slot + 1) * rows)
                marks = emb[at, width:].astype(jnp.float32).astype(jnp.int32)
                behind, label = marks[:, 0:1], marks[:, 1:2]
                hit = column == label
                for plane in range(WINDOW_PLANES + 1):
                    distance = ahead + 8 * plane - (2 * y + core)
                    columns = slice(plane * rows, (plane + 1) * rows)
                    tile = chance[(slot - first) * rows : (slot - first + 1) * rows, columns]
                    tile = tile - jnp.where(hit & (behind == distance), 1.0, 0.0)
                    if plane in (0, WINDOW_PLANES):
                        tile = tile * jnp.where((distance >= 0) & (distance < 8 * WINDOW_PLANES), 1.0, 0.0)
                    coeff_ref[at, columns] = tile.astype(jnp.bfloat16)
    far_ref[...] = text_sum(own_coeff, other_coeff, own_emb, other_emb, WINDOW_PLANES).astype(far_ref.dtype)


def sum_pairs(where_ref, own_coeff, other_coeff, own_emb, other_emb, text_emb, *outs):
    rows = own_emb.shape[0] // 4
    text_sums, kept, sent = outs[:4], outs[4:8], outs[8:]
    for plane in range(WINDOW_PLANES):
        text_sums[plane][...] = text_sum(own_coeff, other_coeff, own_emb, other_emb, plane)
    for first in (0, 2):
        at = slice(first * rows, (first + 2) * rows)
        both = jnp.dot(own_coeff[at, :], text_emb[...], preferred_element_type=jnp.float32)
        kept[first][...] = both[:rows]
        kept[first + 1][...] = both[rows:]
        both = jnp.dot(other_coeff[at, :], text_emb[...], preferred_element_type=jnp.float32)
        sent[first][...] = both[:rows].astype(jnp.bfloat16)
        sent[first + 1][...] = both[rows:].astype(jnp.bfloat16)


def finish(where_ref, sum_ref, unit_ref, norm_ref, weight_ref, *refs):
    arrived, grad_ref = refs[:-1], refs[-1]
    total = sum_ref[...]
    for one in arrived:
        total = total + one[...].astype(jnp.float32)
    draw = unproject(unit_ref[...], norm_ref[:, 0:1], logit_scale * total)
    grad_ref[...] = lax.dot_general(draw, weight_ref[...], contract_last, preferred_element_type=jnp.float32)


def normalize(raw):
    norm = jnp.sqrt(jnp.sum(raw * raw, axis=-1, keepdims=True) + eps)
    return (raw * (1.0 / norm), norm)


def unproject(unit, norm, grad):
    inner = jnp.sum(unit * grad, axis=-1, keepdims=True)
    return ((grad - unit * inner) * (1.0 / norm)).astype(jnp.bfloat16)


def per_device(image_features, text_features, projections, labels):
    rows, width = image_features.shape
    x, z, y, c = (lax.axis_index(a) for a in AXES)
    index = lax.axis_index(AXES)
    tied = lax.optimization_barrier

    marks = jnp.stack([(index - labels // rows) % 256, labels % rows], axis=1).astype(image_features.dtype)
    marked = jnp.concatenate([image_features, jnp.pad(marks, ((0, 0), (0, 126)))], axis=1)

    hop1 = blocks_behind(text_features, 8)
    unit, hop1, marked = tied((start_weights(projections), hop1, marked))
    hop2 = blocks_behind(hop1, 8)
    around = [along(marked, "y", -1), along(marked, "y", 2), along(marked, "y", 1)]
    unit, hop2, *around = tied((spread_units(unit), hop2, *around))
    hop3 = blocks_behind(hop2, 8)
    hop3, *near = tied((hop3, *gather_near(unit)))
    block = join_units(near)
    hop4 = blocks_behind(hop3, 8)
    pieces = [block] + [crosswise(block, "x", d) for d in (1, 2, 3)]
    swapped = along(block, "c", 1)
    hop4, swapped, *pieces = tied((hop4, swapped, *pieces))
    pieces = pieces + [swapped] + [along(piece, "c", 1) for piece in pieces[1:]]
    images, texts = [marked, *around], [text_features, hop1, hop2, hop3, hop4]

    whole = like(4 * block.shape[0], width, block.dtype)
    first_x, first_y = (x + 1) % 4, y
    where = (c, jnp.where(c == 0, first_x, first_y), jnp.where(c == 0, first_y, first_x), y)
    wide, narrow = like(rows, width, jnp.float32), like(rows, 128, jnp.float32)
    low = jnp.bfloat16
    sems = [pltpu.SemaphoreType.DMA((4,))]
    image_weight, image_emb, image_unit, image_norm = on_device(
        embed_images, where, pieces + images, [whole, like(4 * rows, width + 128, low), wide, narrow], sems,
        flops=8 * rows * width * width, vmem=16, anywhere=8,
    )
    other_emb = along(image_emb, "c", 1)
    text_weight, text_emb, text_unit, text_norm = on_device(
        embed_texts, where, pieces + texts, [whole, like(5 * rows, width, low), wide, narrow], sems,
        flops=10 * rows * width * width, vmem=16, anywhere=8,
    )
    coeff, other_coeff, far = on_device(
        weigh_pairs, where, [image_emb, other_emb, text_emb],
        [like(4 * rows, 5 * rows, low), like(4 * rows, 5 * rows, low), like(rows, width, low)],
        flops=96 * rows * rows * width, vmem=20,
    )
    far = blocks_behind(far, -8)
    sums = on_device(
        sum_pairs, (y,), [coeff, other_coeff, image_emb, other_emb, text_emb],
        [wide] * 8 + [like(rows, width, low)] * 4,
        flops=2 * 72 * rows * rows * width, vmem=20,
    )
    text_sums, kept, sent = sums[:4], sums[4:8], sums[8:]

    far = blocks_behind((far.astype(jnp.float32) + text_sums[3]).astype(low), -8)
    chip = [kept[dy] + along(sent[dy], "c", 1).astype(jnp.float32) for dy in range(4)]
    arrived = [along(chip[dy].astype(low), "y", steps) for dy, steps in ((1, 1), (2, 2), (3, -1))]
    far, arrived[0] = tied((far, arrived[0]))
    far = blocks_behind((far.astype(jnp.float32) + text_sums[2]).astype(low), -8)
    far, arrived[2] = tied((far, arrived[2]))
    far = blocks_behind((far.astype(jnp.float32) + text_sums[1]).astype(low), -8)
    flops = 2 * rows * width * width
    (image_grad,) = on_device(finish, (y,), [chip[0], image_unit, image_norm, image_weight, *arrived], [wide], flops=flops, vmem=16)
    (text_grad,) = on_device(finish, (y,), [text_sums[0], text_unit, text_norm, text_weight, far], [wide], flops=flops, vmem=16)
    return (image_grad, text_grad)


def solution(mesh):
    fine = Mesh(mesh.devices.reshape(SIZES), AXES)
    rows = P(AXES, None)
    return jax.shard_map(
        per_device,
        mesh=fine,
        in_specs=(rows, rows, rows, P(AXES)),
        out_specs=(rows, rows),
        check_vma=False,
    )
```

```python
import jax
import jax.numpy as jnp
from jax import lax
from jax.experimental import pallas as pl
from jax.experimental.pallas import tpu as pltpu
from jax.sharding import Mesh, PartitionSpec as P

AXES = ("x", "z", "y", "c")
SIZES = (4, 8, 4, 2)
WINDOW_PLANES = 4

logit_scale = 10.0
logit_bias = -2.0
eps = 1e-06
contract_last = (((1,), (1,)), ((), ()))
contract_first = (((0,), (0,)), ((), ()))


def along(value, axis, steps):
    count = lax.axis_size(axis)
    return lax.ppermute(value, axis, [(i, (i + steps) % count) for i in range(count)])


def blocks_behind(value, steps):
    return lax.ppermute(value, AXES, [(i, (i + steps) % 256) for i in range(256)])


def device(x, z, y, c):
    return ((x * 8 + z) * 4 + y) * 2 + c


def everyone():
    return [(x, z, y, c) for x in range(4) for z in range(8) for y in range(4) for c in range(2)]


def crosswise(value, core0_axis, steps):
    pairs = []
    for x, z, y, c in everyone():
        if (core0_axis == "x") == (c == 0):
            source = device((x + steps) % 4, z, y, c)
        else:
            source = device(x, z, (y + steps) % 4, c)
        pairs.append((source, device(x, z, y, c)))
    return lax.ppermute(value, AXES, pairs)


def order_shards(where_ref, *refs):
    chips, out_ref, wide_ref = refs[:4], refs[4], refs[5]
    height = chips[0].shape[0] // 2
    for n in range(8):
        slot = 2 * lax.rem(where_ref[0] + n // 2, 4) + lax.rem(where_ref[1] + n % 2, 2)
        shard = chips[n // 2][...].astype(jnp.float32)
        for row in range(height):
            at = n % 2 * height + row
            wide_ref[pl.ds(slot * height + row, 1), :] = shard[at : at + 1]
    out_ref[...] = wide_ref[...].astype(out_ref.dtype)


def order_units(where_ref, *refs):
    units, out_ref, wide_ref = refs[:4], refs[4], refs[5]
    height = units[0].shape[0]
    for n, unit_ref in enumerate(units):
        at = pl.multiple_of(lax.rem(where_ref[0] + n, 4) * height, 8)
        wide_ref[pl.ds(at, height), :] = unit_ref[...].astype(jnp.float32)
    out_ref[...] = wide_ref[...].astype(out_ref.dtype)


def on_device(body, where, arrays, outs, scratch=(), flops=0, vmem=8, anywhere=0):
    out_bytes = sum(o.size * o.dtype.itemsize for o in outs) + sum(v.size * v.dtype.itemsize for v in arrays)
    return pl.pallas_call(
        body,
        out_shape=outs,
        in_specs=[pl.BlockSpec(memory_space=pltpu.SMEM)]
        + [pl.BlockSpec(memory_space=pl.ANY)] * min(anywhere, 8)
        + [pl.BlockSpec(memory_space=pltpu.HBM)] * max(anywhere - 8, 0)
        + [pl.BlockSpec(memory_space=pltpu.VMEM)] * (len(arrays) - anywhere),
        out_specs=[pl.BlockSpec(memory_space=pltpu.VMEM)] * len(outs),
        scratch_shapes=list(scratch),
        compiler_params=pltpu.CompilerParams(vmem_limit_bytes=vmem << 20),
        cost_estimate=pl.CostEstimate(flops=flops, bytes_accessed=out_bytes, transcendentals=0),
    )(jnp.stack(where).astype(jnp.int32), *arrays)


def like(rows, width, dtype):
    return jax.ShapeDtypeStruct((rows, width), dtype)


def unit_place(x, z, y, c):
    high, low = (x % 2) * 2 + z // 4, z % 4
    tx, ty = ((high + 3) % 4, low) if x < 2 else (low, high)
    far = [z, z + 1, z - 1, z + 2, z - 2, z + 3, z - 3, z + 4]
    rank = 2 * {0: 3, 1: 1, 3: 2, 2: 0}[(y - ty) % 4] + c
    return (tx, far[rank] % 8, ty, x // 2)


def start_weights(shard):
    y, c = lax.axis_index("y"), lax.axis_index("c")
    chip = jnp.concatenate([shard, along(shard, "c", 1)])
    chips = [chip, along(chip, "y", -1), along(chip, "y", 2), along(chip, "y", 1)]
    height, width = 4 * chip.shape[0], chip.shape[1]
    (unit,) = on_device(
        order_shards, (y, c), chips, [like(height, width, shard.dtype)], [pltpu.VMEM((height, width), jnp.float32)]
    )
    return unit


def spread_units(unit):
    pairs = [(device(*source), device(*unit_place(*source))) for source in everyone()]
    return lax.ppermute(unit, AXES, pairs)


def gather_near(unit):
    return [unit] + [crosswise(unit, "y", d) for d in (1, 2, 3)]


def join_units(near):
    x, y, c = lax.axis_index("x"), lax.axis_index("y"), lax.axis_index("c")
    height, width = 4 * near[0].shape[0], near[0].shape[1]
    (block,) = on_device(
        order_units, (jnp.where(c == 0, y, x),), near, [like(height, width, near[0].dtype)],
        [pltpu.VMEM((height, width), jnp.float32)],
    )
    return block


def place(where_ref, on_core0, pieces, weight, sems):
    for core_is_0 in (True, False):

        @pl.when((where_ref[0] == 0) if core_is_0 else (where_ref[0] != 0))
        def _():
            own = core_is_0 == on_core0
            block = pieces[0].shape[0]
            first = where_ref[1] if own else where_ref[2]
            copies = []
            for n in range(4):
                at = pl.multiple_of(lax.rem(first + n, 4) * block, 32)
                piece = pieces[n if own else 4 + n]
                copies.append(pltpu.make_async_copy(piece, weight.at[pl.ds(at, block)], sems.at[n]))
            for copy in copies:
                copy.start()
            for copy in copies:
                copy.wait()


def bring(sources, held, sems):
    rows = sources[0].shape[0]
    copies = [
        pltpu.make_async_copy(source, held.at[pl.ds(n * rows, rows)], sems.at[n]) for n, source in enumerate(sources)
    ]
    for copy in copies:
        copy.start()
    return copies


def embed(held, weight, emb, unit_ref, norm_ref):
    rows, width = unit_ref.shape
    for first in range(0, held.shape[0], 2 * rows):
        at = slice(first, min(first + 2 * rows, held.shape[0]))
        unit, norm = normalize(jnp.dot(held[at, :width], weight[...], preferred_element_type=jnp.float32))
        emb[at, :width] = unit.astype(jnp.bfloat16)
        if first == 0:
            unit_ref[...] = unit[:rows]
            norm_ref[...] = jnp.broadcast_to(norm[:rows], norm_ref.shape)


def embed_images(where_ref, *refs):
    weight, emb, unit_ref, norm_ref, sems, held, held_sems = refs[12:]
    copies = bring(refs[8:12], held, held_sems)
    place(where_ref, True, refs[:8], weight, sems)
    for copy in copies:
        copy.wait()
    embed(held, weight, emb, unit_ref, norm_ref)
    width = unit_ref.shape[1]
    emb[:, width:] = held[:, width:]


def embed_texts(where_ref, *refs):
    weight, emb, unit_ref, norm_ref, sems, held, held_sems = refs[13:]
    copies = bring(refs[8:13], held, held_sems)
    place(where_ref, False, refs[:8], weight, sems)
    for copy in copies:
        copy.wait()
    embed(held, weight, emb, unit_ref, norm_ref)


def text_sum(own_coeff, other_coeff, own_emb, other_emb, plane):
    width = own_emb.shape[1] - 128
    rows = own_emb.shape[0] // 4
    total = 0.0
    for coeff, emb in ((own_coeff, own_emb), (other_coeff, other_emb)):
        total = total + lax.dot_general(
            coeff[:, plane * rows : (plane + 1) * rows], emb[:, :width], contract_first,
            preferred_element_type=jnp.float32,
        )
    return total


def weigh(where_ref, kind, emb, text_emb, coeff_ref, planes):
    core, y = where_ref[0], where_ref[1]
    rows, width = emb.shape[0] // 4, text_emb.shape[1]
    column = lax.broadcasted_iota(jnp.int32, (rows, rows), 1)
    texts = text_emb[planes[0] * rows : (planes[-1] + 1) * rows, :]
    for first in (0, 2):
        logits = logit_bias + logit_scale * lax.dot_general(
            emb[first * rows : (first + 2) * rows, :width], texts, contract_last, preferred_element_type=jnp.float32
        )
        chance = jax.nn.sigmoid(logits)
        for slot in (first, first + 1):
            ahead = 2 * lax.rem(y + slot, 4) + lax.rem(core + kind, 2)
            at = slice(slot * rows, (slot + 1) * rows)
            marks = emb[at, width:].astype(jnp.float32).astype(jnp.int32)
            behind, label = marks[:, 0:1], marks[:, 1:2]
            hit = column == label
            for n, plane in enumerate(planes):
                distance = ahead + 8 * plane - (2 * y + core)
                columns = slice(n * rows, (n + 1) * rows)
                tile = chance[(slot - first) * rows : (slot - first + 1) * rows, columns]
                tile = tile - jnp.where(hit & (behind == distance), 1.0, 0.0)
                if plane in (0, WINDOW_PLANES):
                    tile = tile * jnp.where((distance >= 0) & (distance < 8 * WINDOW_PLANES), 1.0, 0.0)
                coeff_ref[at, columns] = tile.astype(jnp.bfloat16)


def sum_far(where_ref, own_emb, other_emb, text_emb, own_coeff, other_coeff, third_ref, far_ref):
    planes = (WINDOW_PLANES - 1, WINDOW_PLANES)
    weigh(where_ref, 0, own_emb, text_emb, own_coeff, planes)
    weigh(where_ref, 1, other_emb, text_emb, other_coeff, planes)
    for n, sum_ref in enumerate((third_ref, far_ref)):
        sum_ref[...] = text_sum(own_coeff, other_coeff, own_emb, other_emb, n).astype(sum_ref.dtype)


def sum_pairs(where_ref, own_far, other_far, own_emb, other_emb, text_emb, *refs):
    rows = own_emb.shape[0] // 4
    text_sums, kept, sent = refs[:3], refs[3:7], refs[7:11]
    own_coeff, other_coeff = refs[11:]
    planes = tuple(range(WINDOW_PLANES - 1))
    near = len(planes) * rows
    weigh(where_ref, 0, own_emb, text_emb, own_coeff, planes)
    weigh(where_ref, 1, other_emb, text_emb, other_coeff, planes)
    for plane in planes:
        text_sums[plane][...] = text_sum(own_coeff, other_coeff, own_emb, other_emb, plane)

    def image_sum(coeff, far, at):
        total = jnp.dot(coeff[at, :], text_emb[:near, :], preferred_element_type=jnp.float32)
        return total + jnp.dot(far[at, :], text_emb[near:, :], preferred_element_type=jnp.float32)

    for first in (0, 2):
        at = slice(first * rows, (first + 2) * rows)
        both = image_sum(own_coeff, own_far, at)
        kept[first][...] = both[:rows]
        kept[first + 1][...] = both[rows:]
        both = image_sum(other_coeff, other_far, at)
        sent[first][...] = both[:rows].astype(jnp.bfloat16)
        sent[first + 1][...] = both[rows:].astype(jnp.bfloat16)


def finish(where_ref, sum_ref, unit_ref, norm_ref, weight_ref, *refs):
    arrived, grad_ref = refs[:-1], refs[-1]
    total = sum_ref[...]
    for one in arrived:
        total = total + one[...].astype(jnp.float32)
    draw = unproject(unit_ref[...], norm_ref[:, 0:1], logit_scale * total)
    grad_ref[...] = lax.dot_general(draw, weight_ref[...], contract_last, preferred_element_type=jnp.float32)


def last_step_home(value):
    pairs = []
    for x, z, y, c in everyone():
        first_z = (z - 3) % 8
        pairs.append((device(x, z, y, c), device((x if first_z >= 4 else x - 1) % 4, (z + 1) % 8, y, c)))
    return lax.ppermute(value, AXES, pairs)


def normalize(raw):
    norm = jnp.sqrt(jnp.sum(raw * raw, axis=-1, keepdims=True) + eps)
    return (raw * (1.0 / norm), norm)


def unproject(unit, norm, grad):
    inner = jnp.sum(unit * grad, axis=-1, keepdims=True)
    return ((grad - unit * inner) * (1.0 / norm)).astype(jnp.bfloat16)


def per_device(image_features, text_features, projections, labels):
    rows, width = image_features.shape
    x, z, y, c = (lax.axis_index(a) for a in AXES)
    index = lax.axis_index(AXES)
    tied = lax.optimization_barrier

    marks = jnp.stack([(index - labels // rows) % 256, labels % rows], axis=1).astype(image_features.dtype)
    marked = jnp.concatenate([image_features, jnp.pad(marks, ((0, 0), (0, 126)))], axis=1)

    hop1 = blocks_behind(text_features, 8)
    unit, hop1, marked = tied((start_weights(projections), hop1, marked))
    hop2 = blocks_behind(hop1, 8)
    around = [along(marked, "y", -1), along(marked, "y", 2), along(marked, "y", 1)]
    unit, hop2, *around = tied((spread_units(unit), hop2, *around))
    hop3 = blocks_behind(hop2, 8)
    hop3, *near = tied((hop3, *gather_near(unit)))
    block = join_units(near)
    hop4 = blocks_behind(hop3, 8)
    pieces = [block] + [crosswise(block, "x", d) for d in (1, 2, 3)]
    swapped = along(block, "c", 1)
    hop4, swapped, *pieces = tied((hop4, swapped, *pieces))
    pieces = pieces + [swapped] + [along(piece, "c", 1) for piece in pieces[1:]]
    images, texts = [marked, *around], [text_features, hop1, hop2, hop3, hop4]

    whole = like(4 * block.shape[0], width, block.dtype)
    first_x, first_y = (x + 1) % 4, y
    where = (c, jnp.where(c == 0, first_x, first_y), jnp.where(c == 0, first_y, first_x), y)
    wide, narrow = like(rows, width, jnp.float32), like(rows, 128, jnp.float32)
    low = jnp.bfloat16
    sems = [pltpu.SemaphoreType.DMA((4,))]
    image_weight, image_emb, image_unit, image_norm = on_device(
        embed_images, where, pieces + images, [whole, like(4 * rows, width + 128, low), wide, narrow],
        [*sems, pltpu.VMEM((4 * rows, width + 128), low), pltpu.SemaphoreType.DMA((4,))],
        flops=8 * rows * width * width, vmem=56, anywhere=12,
    )
    other_emb = along(image_emb, "c", 1)
    text_weight, text_emb, text_unit, text_norm = on_device(
        embed_texts, where, pieces + texts, [whole, like(5 * rows, width, low), wide, narrow],
        [*sems, pltpu.VMEM((5 * rows, width), low), pltpu.SemaphoreType.DMA((5,))],
        flops=10 * rows * width * width, vmem=56, anywhere=13,
    )
    own_far, other_far, third, far = on_device(
        sum_far, (c, y), [image_emb, other_emb, text_emb],
        [like(4 * rows, 2 * rows, low)] * 2 + [like(rows, width, low)] * 2,
        flops=64 * rows * rows * width, vmem=16,
    )
    home = along(far, "z", 3)
    third = blocks_behind(third, -8)
    sums = on_device(
        sum_pairs, (c, y), [own_far, other_far, image_emb, other_emb, text_emb],
        [wide] * 7 + [like(rows, width, low)] * 4, [pltpu.VMEM((4 * rows, 3 * rows), low)] * 2,
        flops=2 * 88 * rows * rows * width, vmem=20,
    )
    text_sums, kept, sent = sums[:3], sums[3:7], sums[7:]

    second = blocks_behind((third.astype(jnp.float32) + text_sums[2]).astype(low), -8)
    chip = [kept[dy] + along(sent[dy], "c", 1).astype(jnp.float32) for dy in range(4)]
    arrived = [along(chip[dy].astype(low), "y", steps) for dy, steps in ((1, 1), (2, 2), (3, -1))]
    home = last_step_home(home)
    second, arrived[0] = tied((second, arrived[0]))
    first = blocks_behind((second.astype(jnp.float32) + text_sums[1]).astype(low), -8)
    flops = 2 * rows * width * width
    (image_grad,) = on_device(finish, (y,), [chip[0], image_unit, image_norm, image_weight, *arrived], [wide], flops=flops, vmem=16)
    (text_grad,) = on_device(finish, (y,), [text_sums[0], text_unit, text_norm, text_weight, first, home], [wide], flops=flops, vmem=16)
    return (image_grad, text_grad)


def solution(mesh):
    fine = Mesh(mesh.devices.reshape(SIZES), AXES)
    rows = P(AXES, None)
    return jax.shard_map(
        per_device,
        mesh=fine,
        in_specs=(rows, rows, rows, P(AXES)),
        out_specs=(rows, rows),
        check_vma=False,
    )
```

```python
import jax
import jax.numpy as jnp
from jax import lax
from jax.experimental import pallas as pl
from jax.experimental.pallas import tpu as pltpu
from jax.sharding import Mesh, PartitionSpec as P

AXES = ("x", "z", "y", "c")
SIZES = (4, 8, 4, 2)
WINDOW_PLANES = 4

logit_scale = 10.0
logit_bias = -2.0
eps = 1e-06
contract_last = (((1,), (1,)), ((), ()))
contract_first = (((0,), (0,)), ((), ()))


def along(value, axis, steps):
    count = lax.axis_size(axis)
    return lax.ppermute(value, axis, [(i, (i + steps) % count) for i in range(count)])


def blocks_behind(value, steps):
    return lax.ppermute(value, AXES, [(i, (i + steps) % 256) for i in range(256)])


def device(x, z, y, c):
    return ((x * 8 + z) * 4 + y) * 2 + c


def everyone():
    return [(x, z, y, c) for x in range(4) for z in range(8) for y in range(4) for c in range(2)]


def crosswise(value, core0_axis, steps):
    pairs = []
    for x, z, y, c in everyone():
        if (core0_axis == "x") == (c == 0):
            source = device((x + steps) % 4, z, y, c)
        else:
            source = device(x, z, (y + steps) % 4, c)
        pairs.append((source, device(x, z, y, c)))
    return lax.ppermute(value, AXES, pairs)


def order_shards(where_ref, *refs):
    chips, out_ref, wide_ref = refs[:4], refs[4], refs[5]
    height = chips[0].shape[0] // 2
    for n in range(8):
        slot = 2 * lax.rem(where_ref[0] + n // 2, 4) + lax.rem(where_ref[1] + n % 2, 2)
        shard = chips[n // 2][...].astype(jnp.float32)
        for row in range(height):
            at = n % 2 * height + row
            wide_ref[pl.ds(slot * height + row, 1), :] = shard[at : at + 1]
    out_ref[...] = wide_ref[...].astype(out_ref.dtype)


def order_units(where_ref, *refs):
    units, out_ref, wide_ref = refs[:4], refs[4], refs[5]
    height = units[0].shape[0]
    for n, unit_ref in enumerate(units):
        at = pl.multiple_of(lax.rem(where_ref[0] + n, 4) * height, 8)
        wide_ref[pl.ds(at, height), :] = unit_ref[...].astype(jnp.float32)
    out_ref[...] = wide_ref[...].astype(out_ref.dtype)


def on_device(body, where, arrays, outs, scratch=(), flops=0, vmem=8, anywhere=0):
    out_bytes = sum(o.size * o.dtype.itemsize for o in outs) + sum(v.size * v.dtype.itemsize for v in arrays)
    return pl.pallas_call(
        body,
        out_shape=outs,
        in_specs=[pl.BlockSpec(memory_space=pltpu.SMEM)]
        + [pl.BlockSpec(memory_space=pl.ANY)] * min(anywhere, 8)
        + [pl.BlockSpec(memory_space=pltpu.HBM)] * max(anywhere - 8, 0)
        + [pl.BlockSpec(memory_space=pltpu.VMEM)] * (len(arrays) - anywhere),
        out_specs=[pl.BlockSpec(memory_space=pltpu.VMEM)] * len(outs),
        scratch_shapes=list(scratch),
        compiler_params=pltpu.CompilerParams(vmem_limit_bytes=vmem << 20),
        cost_estimate=pl.CostEstimate(flops=flops, bytes_accessed=out_bytes, transcendentals=0),
    )(jnp.stack(where).astype(jnp.int32), *arrays)


def like(rows, width, dtype):
    return jax.ShapeDtypeStruct((rows, width), dtype)


def unit_place(x, z, y, c):
    high, low = (x % 2) * 2 + z // 4, z % 4
    tx, ty = ((high + 3) % 4, low) if x < 2 else (low, high)
    far = [z, z + 1, z - 1, z + 2, z - 2, z + 3, z - 3, z + 4]
    rank = 2 * {0: 3, 1: 1, 3: 2, 2: 0}[(y - ty) % 4] + c
    return (tx, far[rank] % 8, ty, x // 2)


def start_weights(shard):
    y, c = lax.axis_index("y"), lax.axis_index("c")
    chip = jnp.concatenate([shard, along(shard, "c", 1)])
    chips = [chip, along(chip, "y", -1), along(chip, "y", 2), along(chip, "y", 1)]
    height, width = 4 * chip.shape[0], chip.shape[1]
    (unit,) = on_device(
        order_shards, (y, c), chips, [like(height, width, shard.dtype)], [pltpu.VMEM((height, width), jnp.float32)]
    )
    return unit


def spread_units(unit):
    pairs = [(device(*source), device(*unit_place(*source))) for source in everyone()]
    return lax.ppermute(unit, AXES, pairs)


def gather_near(unit):
    return [unit] + [crosswise(unit, "y", d) for d in (1, 2, 3)]


def join_units(near):
    x, y, c = lax.axis_index("x"), lax.axis_index("y"), lax.axis_index("c")
    height, width = 4 * near[0].shape[0], near[0].shape[1]
    (block,) = on_device(
        order_units, (jnp.where(c == 0, y, x),), near, [like(height, width, near[0].dtype)],
        [pltpu.VMEM((height, width), jnp.float32)],
    )
    return block


def place(where_ref, on_core0, pieces, weight, sems):
    for core_is_0 in (True, False):

        @pl.when((where_ref[0] == 0) if core_is_0 else (where_ref[0] != 0))
        def _():
            own = core_is_0 == on_core0
            block = pieces[0].shape[0]
            first = where_ref[1] if own else where_ref[2]
            copies = []
            for n in range(4):
                at = pl.multiple_of(lax.rem(first + n, 4) * block, 32)
                piece = pieces[n if own else 4 + n]
                copies.append(pltpu.make_async_copy(piece, weight.at[pl.ds(at, block)], sems.at[n]))
            for copy in copies:
                copy.start()
            for copy in copies:
                copy.wait()


def bring(sources, held, sems):
    rows = sources[0].shape[0]
    copies = [
        pltpu.make_async_copy(source, held.at[pl.ds(n * rows, rows)], sems.at[n]) for n, source in enumerate(sources)
    ]
    for copy in copies:
        copy.start()
    return copies


def embed(held, weight, emb, unit_ref, norm_ref):
    rows, width = unit_ref.shape
    for first in range(0, held.shape[0], 2 * rows):
        at = slice(first, min(first + 2 * rows, held.shape[0]))
        unit, norm = normalize(jnp.dot(held[at, :width], weight[...], preferred_element_type=jnp.float32))
        emb[at, :width] = unit.astype(jnp.bfloat16)
        if first == 0:
            unit_ref[...] = unit[:rows]
            norm_ref[...] = jnp.broadcast_to(norm[:rows], norm_ref.shape)


def embed_images(where_ref, *refs):
    weight, emb, unit_ref, norm_ref, sems, held, held_sems = refs[12:]
    copies = bring(refs[8:12], held, held_sems)
    place(where_ref, True, refs[:8], weight, sems)
    for copy in copies:
        copy.wait()
    embed(held, weight, emb, unit_ref, norm_ref)
    width = unit_ref.shape[1]
    emb[:, width:] = held[:, width:]


def embed_texts(where_ref, *refs):
    weight, emb, unit_ref, norm_ref, sems, held, held_sems = refs[13:]
    copies = bring(refs[8:13], held, held_sems)
    place(where_ref, False, refs[:8], weight, sems)
    for copy in copies:
        copy.wait()
    embed(held, weight, emb, unit_ref, norm_ref)


def text_sum(own_coeff, other_coeff, own_emb, other_emb, plane):
    width = own_emb.shape[1] - 128
    rows = own_emb.shape[0] // 4
    total = 0.0
    for coeff, emb in ((own_coeff, own_emb), (other_coeff, other_emb)):
        total = total + lax.dot_general(
            coeff[:, plane * rows : (plane + 1) * rows], emb[:, :width], contract_first,
            preferred_element_type=jnp.float32,
        )
    return total


def weigh(where_ref, kind, emb, text_emb, coeff_ref, planes):
    core, y = where_ref[0], where_ref[1]
    rows, width = emb.shape[0] // 4, text_emb.shape[1]
    column = lax.broadcasted_iota(jnp.int32, (rows, rows), 1)
    texts = text_emb[planes[0] * rows : (planes[-1] + 1) * rows, :]
    for first in (0, 2):
        logits = logit_bias + logit_scale * lax.dot_general(
            emb[first * rows : (first + 2) * rows, :width], texts, contract_last, preferred_element_type=jnp.float32
        )
        chance = jax.nn.sigmoid(logits)
        for slot in (first, first + 1):
            ahead = 2 * lax.rem(y + slot, 4) + lax.rem(core + kind, 2)
            at = slice(slot * rows, (slot + 1) * rows)
            marks = emb[at, width:].astype(jnp.float32).astype(jnp.int32)
            behind, label = marks[:, 0:1], marks[:, 1:2]
            hit = column == label
            for n, plane in enumerate(planes):
                distance = ahead + 8 * plane - (2 * y + core)
                columns = slice(n * rows, (n + 1) * rows)
                tile = chance[(slot - first) * rows : (slot - first + 1) * rows, columns]
                tile = tile - jnp.where(hit & (behind == distance), 1.0, 0.0)
                if plane in (0, WINDOW_PLANES):
                    tile = tile * jnp.where((distance >= 0) & (distance < 8 * WINDOW_PLANES), 1.0, 0.0)
                coeff_ref[at, columns] = tile.astype(jnp.bfloat16)


def sum_far(where_ref, own_emb, other_emb, text_emb, own_coeff, other_coeff, third_ref, far_ref):
    planes = (WINDOW_PLANES - 1, WINDOW_PLANES)
    weigh(where_ref, 0, own_emb, text_emb, own_coeff, planes)
    weigh(where_ref, 1, other_emb, text_emb, other_coeff, planes)
    for n, sum_ref in enumerate((third_ref, far_ref)):
        sum_ref[...] = text_sum(own_coeff, other_coeff, own_emb, other_emb, n).astype(sum_ref.dtype)


def sum_pairs(where_ref, own_far, other_far, own_emb, other_emb, text_emb, *refs):
    rows = own_emb.shape[0] // 4
    text_sums, kept, sent = refs[:3], refs[3:7], refs[7:11]
    own_coeff, other_coeff = refs[11:]
    planes = tuple(range(WINDOW_PLANES - 1))
    near = len(planes) * rows
    weigh(where_ref, 0, own_emb, text_emb, own_coeff, planes)
    weigh(where_ref, 1, other_emb, text_emb, other_coeff, planes)
    for plane in planes:
        text_sums[plane][...] = text_sum(own_coeff, other_coeff, own_emb, other_emb, plane)

    def image_sum(coeff, far, at):
        total = jnp.dot(coeff[at, :], text_emb[:near, :], preferred_element_type=jnp.float32)
        return total + jnp.dot(far[at, :], text_emb[near:, :], preferred_element_type=jnp.float32)

    for first in (0, 2):
        at = slice(first * rows, (first + 2) * rows)
        both = image_sum(own_coeff, own_far, at)
        kept[first][...] = both[:rows]
        kept[first + 1][...] = both[rows:]
        both = image_sum(other_coeff, other_far, at)
        sent[first][...] = both[:rows].astype(jnp.bfloat16)
        sent[first + 1][...] = both[rows:].astype(jnp.bfloat16)


def finish(where_ref, sum_ref, unit_ref, norm_ref, weight_ref, *refs):
    arrived, grad_ref = refs[:-1], refs[-1]
    total = sum_ref[...]
    for one in arrived:
        total = total + one[...].astype(jnp.float32)
    draw = unproject(unit_ref[...], norm_ref[:, 0:1], logit_scale * total)
    grad_ref[...] = lax.dot_general(draw, weight_ref[...], contract_last, preferred_element_type=jnp.float32)


def last_step_home(value):
    pairs = []
    for x, z, y, c in everyone():
        first_z = (z - 3) % 8
        pairs.append((device(x, z, y, c), device((x if first_z >= 4 else x - 1) % 4, (z + 1) % 8, y, c)))
    return lax.ppermute(value, AXES, pairs)


def normalize(raw):
    norm = jnp.sqrt(jnp.sum(raw * raw, axis=-1, keepdims=True) + eps)
    return (raw * (1.0 / norm), norm)


def unproject(unit, norm, grad):
    inner = jnp.sum(unit * grad, axis=-1, keepdims=True)
    return ((grad - unit * inner) * (1.0 / norm)).astype(jnp.bfloat16)


def per_device(image_features, text_features, projections, labels):
    rows, width = image_features.shape
    x, z, y, c = (lax.axis_index(a) for a in AXES)
    index = lax.axis_index(AXES)
    tied = lax.optimization_barrier

    marks = jnp.stack([(index - labels // rows) % 256, labels % rows], axis=1).astype(image_features.dtype)
    marked = jnp.concatenate([image_features, jnp.pad(marks, ((0, 0), (0, 126)))], axis=1)

    hop1 = blocks_behind(text_features, 8)
    unit, hop1, marked = tied((start_weights(projections), hop1, marked))
    hop2 = blocks_behind(hop1, 8)
    around = [along(marked, "y", -1), along(marked, "y", 2), along(marked, "y", 1)]
    unit, hop2, *around = tied((spread_units(unit), hop2, *around))
    hop3 = blocks_behind(hop2, 8)
    hop3, *near = tied((hop3, *gather_near(unit)))
    block = join_units(near)
    hop4 = blocks_behind(hop3, 8)
    pieces = [block] + [crosswise(block, "x", d) for d in (1, 2, 3)]
    swapped = along(block, "c", 1)
    hop4, swapped, *pieces = tied((hop4, swapped, *pieces))
    pieces = pieces + [swapped] + [along(piece, "c", 1) for piece in pieces[1:]]
    images, texts = [marked, *around], [text_features, hop1, hop2, hop3, hop4]

    whole = like(4 * block.shape[0], width, block.dtype)
    first_x, first_y = (x + 1) % 4, y
    where = (c, jnp.where(c == 0, first_x, first_y), jnp.where(c == 0, first_y, first_x), y)
    wide, narrow = like(rows, width, jnp.float32), like(rows, 128, jnp.float32)
    low = jnp.bfloat16
    sems = [pltpu.SemaphoreType.DMA((4,))]
    image_weight, image_emb, image_unit, image_norm = on_device(
        embed_images, where, pieces + images, [whole, like(4 * rows, width + 128, low), wide, narrow],
        [*sems, pltpu.VMEM((4 * rows, width + 128), low), pltpu.SemaphoreType.DMA((4,))],
        flops=8 * rows * width * width, vmem=56, anywhere=12,
    )
    other_emb = along(image_emb, "c", 1)
    text_weight, text_emb, text_unit, text_norm = on_device(
        embed_texts, where, pieces + texts, [whole, like(5 * rows, width, low), wide, narrow],
        [*sems, pltpu.VMEM((5 * rows, width), low), pltpu.SemaphoreType.DMA((5,))],
        flops=10 * rows * width * width, vmem=56, anywhere=13,
    )
    own_far, other_far, third, far = on_device(
        sum_far, (c, y), [image_emb, other_emb, text_emb],
        [like(4 * rows, 2 * rows, low)] * 2 + [like(rows, width, low)] * 2,
        flops=64 * rows * rows * width, vmem=16,
    )
    home = along(far, "z", 3)
    third = blocks_behind(third, -8)
    sums = on_device(
        sum_pairs, (c, y), [own_far, other_far, image_emb, other_emb, text_emb],
        [wide] * 7 + [like(rows, width, low)] * 4, [pltpu.VMEM((4 * rows, 3 * rows), low)] * 2,
        flops=2 * 88 * rows * rows * width, vmem=20,
    )
    text_sums, kept, sent = sums[:3], sums[3:7], sums[7:]

    second = blocks_behind((third.astype(jnp.float32) + text_sums[2]).astype(low), -8)
    chip = [kept[dy] + along(sent[dy], "c", 1).astype(jnp.float32) for dy in range(4)]
    arrived = [along(chip[dy].astype(low), "y", steps) for dy, steps in ((1, 1), (2, 2), (3, -1))]
    home = last_step_home(home)
    second, arrived[0] = tied((second, arrived[0]))
    first = blocks_behind((second.astype(jnp.float32) + text_sums[1]).astype(low), -8)
    first, arrived[1] = tied((first, arrived[1]))
    flops = 2 * rows * width * width
    (image_grad,) = on_device(finish, (y,), [chip[0], image_unit, image_norm, image_weight, *arrived], [wide], flops=flops, vmem=16)
    (text_grad,) = on_device(finish, (y,), [text_sums[0], text_unit, text_norm, text_weight, first, home], [wide], flops=flops, vmem=16)
    return (image_grad, text_grad)


def solution(mesh):
    fine = Mesh(mesh.devices.reshape(SIZES), AXES)
    rows = P(AXES, None)
    return jax.shard_map(
        per_device,
        mesh=fine,
        in_specs=(rows, rows, rows, P(AXES)),
        out_specs=(rows, rows),
        check_vma=False,
    )
```
